32 devices in a mesh: groups: 2 (over x), frame: 8 (over z, y), tok: 2 (over core).
Axes of the slice: x: 2, y: 2, z: 4, core: 2. Of those that a mesh axis runs over, the one named last changes fastest.
Arguments:
- video: bfloat16 [32, 512, 1152], P(('groups', 'frame'), 'tok'), parts along dimension 0, may hold values from -6 to 6
- regions: int32 [32, 512], P(('groups', 'frame'), 'tok'), parts along dimension 0, may hold values from 0 to 2
- prev_frame: int32 [32], P('groups'), parts along dimension 0, may hold values from 0 to 14, as said below
- gain_spatial: float32 [1152], replicated, may hold values from 0.7 to 4
- qkv_spatial: bfloat16 [1152, 3456], replicated, may hold values from -0.35355339 to 0.35355339
- out_spatial: bfloat16 [1152, 1152], replicated, may hold values from -1.5 to 1.5
- gain_temporal: float32 [1152], replicated, may hold values from 0.7 to 4
- qkv_temporal: bfloat16 [1152, 3456], replicated, may hold values from -0.35355339 to 0.35355339
- out_temporal: bfloat16 [1152, 1152], replicated, may hold values from -0.75 to 0.75
Outputs:
- result: bfloat16 [32, 512, 1152], P(('groups', 'frame'), 'tok'), parts along dimension 0
The draws below stay inside these ranges and needn't reach their ends.
There are 2 independent parts, one for each index of `groups`. The reference program is written for one: setup_inputs(seed, part) draws one part's arguments, and reference() takes and returns one part's arrays. A program takes and returns all parts, laid end to end along the dimension named above; an argument that names none is the same for every part. Nothing has to cross between parts.
Inputs may be any that keep to these rules, and one draw needn't show every extreme that they name: prev_frame[f] is f - 1 or f - 2 for 2 <= f < 15, f - 1 for f = 15, and 0 for f < 2.
All inputs are finite; a program needn't handle non-finite values.
Results may differ from the reference program's by a relative error of at most 0.014.
The reference program's roundings to bfloat16 on the way count: a program that leaves them out, or rounds other values in their place, can miss the bound.
Values may be sent and summed in bfloat16 or wider, within the bound.
A program may use at most 192 MiB of HBM per device.

```python
import jax
import jax.numpy as jnp
from jax import lax

HEADS = 16
HEAD_DIM = 72
D = 1152
FRAMES = 16
PLACES = 512


def draw_prev_frame(key, part):
    frame_number = jnp.arange(FRAMES, dtype=jnp.int32)
    skipped = jax.random.randint(jax.random.fold_in(key, 7), (FRAMES,), 0, 2, dtype=jnp.int32)
    skipped = jnp.where(frame_number == FRAMES - 1, 0, skipped)
    return jnp.maximum(frame_number - 1 - skipped, 0).astype(jnp.int32)


def gain_draw(key, salt):
    return jax.random.uniform(jax.random.fold_in(key, salt + 4), (D,), jnp.float32, 0.7, 1.3)


def projection_draw(key, salt):
    base = jax.random.truncated_normal(jax.random.fold_in(key, salt + 2), -6.0, 6.0, (D, 3 * D), jnp.float32)
    base = base * D ** (-0.5)
    return base.astype(jnp.bfloat16)


def draw_gain_spatial(key, part):
    return gain_draw(key, 11)


def draw_qkv_spatial(key, part):
    return projection_draw(key, 11)


def draw_gain_temporal(key, part):
    return gain_draw(key, 31)


def draw_qkv_temporal(key, part):
    return projection_draw(key, 31)


def with_ends(values, stream_key, smallest, high):
    longest = values.shape.index(max(values.shape))
    spots = []
    for shift in (0, 1):
        where = [jax.random.randint(jax.random.fold_in(stream_key, axis), (), 0, length) for axis, length in enumerate(values.shape)]
        where[longest] = (where[longest] + shift) % values.shape[longest]
        spots.append(tuple(where))
    return values.at[spots[0]].set(smallest).at[spots[1]].set(high)


def block_levels(key, dims, split, smallest, high):
    def one(dim, blocks):
        heights = jax.random.uniform(jax.random.fold_in(jax.random.fold_in(key, 6), dim), (blocks,), jnp.float32, smallest / len(split), high / len(split))
        return jnp.repeat(jnp.exp(heights), dims[dim] // blocks).reshape((-1,) + (1,) * (len(dims) - dim - 1))

    factor_of = one(*split[0])
    for cut in split[1:]:
        factor_of = factor_of * one(*cut)
    return factor_of


def gaussian(key, extent, deviation, bound, pieces=(), kind=jnp.bfloat16):
    drawn = jax.random.normal(key, extent, jnp.float32) * deviation
    if len(pieces) > 0:
        drawn = block_levels(key, extent, pieces, -0.22, 0.18) * drawn
    return jnp.clip(drawn, min=-bound, max=bound).astype(kind)


def setup_inputs(seed: int = 0, part: int = 0) -> dict:
    arg_keys = jax.random.split(jax.random.key(seed), 10)
    own_keys = jax.random.split(jax.random.fold_in(arg_keys[9], part), 10)
    return {
        "video": gaussian(own_keys[0], (FRAMES, PLACES, D), 1.0, 6.0, ((0, 8), (1, 2))),
        "regions": with_ends(jax.random.randint(own_keys[1], (FRAMES, PLACES), 0, 3), jax.random.fold_in(own_keys[1], 1), 0, 2).astype(jnp.int32),
        "prev_frame": draw_prev_frame(jax.random.fold_in(jax.random.fold_in(arg_keys[9], part), 71), part),
        "gain_spatial": draw_gain_spatial(jax.random.fold_in(arg_keys[9], 71), part),
        "qkv_spatial": draw_qkv_spatial(jax.random.fold_in(arg_keys[9], 71), part),
        "out_spatial": gaussian(arg_keys[5], (D, D), (max(D // 64, 1)) ** -0.5, 1.5),
        "gain_temporal": draw_gain_temporal(jax.random.fold_in(arg_keys[9], 71), part),
        "qkv_temporal": draw_qkv_temporal(jax.random.fold_in(arg_keys[9], 71), part),
        "out_temporal": gaussian(arg_keys[8], (D, D), (max(D // 16, 1)) ** -0.5, 0.75),
    }


def layer_norm(row_data, gain_vector):
    values = row_data.astype(jnp.float32)
    center = values - lax.optimization_barrier(jnp.mean(values, axis=-1, keepdims=True))
    spread = lax.optimization_barrier(jnp.mean(center * center, axis=-1, keepdims=True))
    return (center * lax.rsqrt(spread + 1e-06) * gain_vector).astype(jnp.bfloat16)

def softmax_rows(scores, visible):
    masked = jnp.where(visible, scores, -jnp.inf)
    largest = lax.optimization_barrier(jnp.max(masked, axis=-1, keepdims=True))
    exponent = jnp.exp(masked - largest)
    return (exponent / lax.optimization_barrier(jnp.sum(exponent, axis=-1, keepdims=True))).astype(jnp.bfloat16)

def reference(video, regions, prev_frame, gain_spatial, qkv_spatial, out_spatial, gain_temporal, qkv_temporal, out_temporal):
    frame_total, places, feature = video.shape
    score_scale = HEAD_DIM ** (-0.5)
    row_count = frame_total * places
    normed = layer_norm(video.reshape(row_count, feature), gain_spatial)
    packed = jnp.dot(normed, qkv_spatial, preferred_element_type=jnp.float32).astype(jnp.bfloat16)
    packed = packed.reshape(frame_total, places, 3, HEADS, HEAD_DIM)
    queries = packed[:, :, 0].astype(jnp.float32)
    keys_all = packed[:, :, 1].astype(jnp.float32)
    values_all = packed[:, :, 2].astype(jnp.float32)
    keep_flag = regions == 0

    def attend_frame(frame_number):
        back_frame = prev_frame[frame_number]
        key_rows = jnp.concatenate([keys_all[frame_number], keys_all[0], keys_all[back_frame]], axis=0)
        value_rows = jnp.concatenate([values_all[frame_number], values_all[0], values_all[back_frame]], axis=0)
        visible = jnp.concatenate([jnp.ones((places,), jnp.bool_), keep_flag[0], keep_flag[back_frame]])
        scores = jnp.einsum('qhd,khd->hqk', queries[frame_number], key_rows) * score_scale
        weights = softmax_rows(scores, visible[None, None, :]).astype(jnp.float32)
        return jnp.einsum('hqk,khd->qhd', weights, value_rows).astype(jnp.bfloat16)
    attended = lax.map(attend_frame, jnp.arange(frame_total, dtype=jnp.int32)).reshape(row_count, feature)
    mixed_rows = (video.reshape(row_count, feature).astype(jnp.float32) + jnp.dot(attended, out_spatial, preferred_element_type=jnp.float32)).astype(jnp.bfloat16)
    normed_t = layer_norm(mixed_rows, gain_temporal)
    packed_t = jnp.dot(normed_t, qkv_temporal, preferred_element_type=jnp.float32).astype(jnp.bfloat16)
    packed_t = packed_t.reshape(frame_total, places, 3, HEADS, HEAD_DIM)
    query_t = packed_t[:, :, 0].astype(jnp.float32)
    key_t = packed_t[:, :, 1].astype(jnp.float32)
    value_t = packed_t[:, :, 2].astype(jnp.float32)
    scores_t = jnp.einsum('fphd,gphd->phfg', query_t, key_t) * score_scale
    open_flag = (regions != 2).T
    visible_t = open_flag[:, None, None, :] | jnp.eye(frame_total, dtype=jnp.bool_)[None, None]
    weights_t = softmax_rows(scores_t, visible_t).astype(jnp.float32)
    temporal_out = jnp.einsum('phfg,gphd->fphd', weights_t, value_t).astype(jnp.bfloat16).reshape(row_count, feature)
    result = (mixed_rows.astype(jnp.float32) + jnp.dot(temporal_out, out_temporal, preferred_element_type=jnp.float32)).astype(jnp.bfloat16)
    return result.reshape(frame_total, places, feature)
```

```python
import functools
import math

import jax
import jax.numpy as jnp
from jax import lax
from jax.experimental import pallas as pl
from jax.experimental.pallas import tpu as pltpu
from jax.sharding import PartitionSpec as P

HEADS = 16
WINDOW = 256
VMEM_BYTES = 56 * 1024 * 1024
NT = (((1,), (1,)), ((), ()))


def shifted(array, axis, by):
    count = lax.axis_size(axis)
    pairs = [(i, i + by) for i in range(count) if 0 <= i + by < count]
    return lax.ppermute(array, axis, pairs)


def from_root(value, axis):
    count = lax.axis_size(axis)
    index = lax.axis_index(axis)
    stride = count // 2
    while stride >= 1:
        pairs = [(i, i + stride) for i in range(0, count, 2 * stride) if i + stride < count]
        arrived = lax.ppermute(value, axis, pairs)
        value = jnp.where(index % (2 * stride) == stride, arrived, value)
        stride //= 2
    return value


def normalize(values, gain):
    center = values - jnp.mean(values, axis=-1, keepdims=True)
    spread = jnp.mean(center * center, axis=-1, keepdims=True)
    return (center * lax.rsqrt(spread + 1e-06) * gain).astype(jnp.bfloat16)


def layer_norm(row_data, gain_vector):
    return normalize(row_data.astype(jnp.float32), gain_vector)


def head_window(head, feature):
    size = feature // HEADS
    start = jnp.minimum((head * size) // 128 * 128, feature - WINDOW)
    start = pl.multiple_of(start, 128)
    column = lax.broadcasted_iota(jnp.int32, (1, WINDOW), 1) + start
    inside = (column >= head * size) & (column < (head + 1) * size)
    return start, inside


def spatial_kernel(
    slots, q_ref, own_ref, first_ref, prem_ref, pown_ref, bfirst_ref, bprev_ref,
    video_ref, wout_ref, out_ref, att_ref, *, scale
):
    feature = video_ref.shape[-1]
    frame = pl.program_id(0)
    remote = slots[frame] < 2
    bias_first = bfirst_ref[0]
    bias_prev = bprev_ref[0]
    att_ref[...] = jnp.zeros_like(att_ref)

    def one(head):
        start, inside = head_window(head, feature)
        cols = pl.ds(start, WINDOW)
        vcols = pl.ds(pl.multiple_of(start + feature, 128), WINDOW)
        q = q_ref[0, :, cols]
        q = jnp.where(inside, q, jnp.zeros_like(q))

        def prev(c):
            return jnp.where(remote, prem_ref[0, :, c], pown_ref[0, :, c])

        dot = functools.partial(
            lax.dot_general, dimension_numbers=NT, preferred_element_type=jnp.float32
        )
        s0 = dot(q, own_ref[0, :, cols]) * scale
        s1 = dot(q, first_ref[0, :, cols]) * scale + bias_first
        s2 = dot(q, prev(cols)) * scale + bias_prev
        m = jnp.max(jnp.maximum(jnp.maximum(s0, s1), s2), axis=-1, keepdims=True)
        p0, p1, p2 = jnp.exp2(s0 - m), jnp.exp2(s1 - m), jnp.exp2(s2 - m)
        total = jnp.sum(p0 + p1 + p2, axis=-1, keepdims=True)
        mul = functools.partial(jnp.dot, preferred_element_type=jnp.float32)
        o = (
            mul(p0.astype(jnp.bfloat16), own_ref[0, :, vcols])
            + mul(p1.astype(jnp.bfloat16), first_ref[0, :, vcols])
            + mul(p2.astype(jnp.bfloat16), prev(vcols))
        ) / total
        att_ref[:, cols] = jnp.where(inside, o.astype(jnp.bfloat16), att_ref[:, cols])

    def pair(i, _):
        one(2 * i)
        one(2 * i + 1)
        return 0

    lax.fori_loop(0, HEADS // 2, pair, 0)
    out_ref[0] = (
        video_ref[0].astype(jnp.float32)
        + jnp.dot(att_ref[...], wout_ref[...], preferred_element_type=jnp.float32)
    ).astype(jnp.bfloat16)


def spatial(slots, packed, kv_own, kv_rem, bias_first, bias_prev, video, wout, scale):
    frames, places, feature = video.shape
    whole = kv_own.shape[1]
    kv = (1, whole, 2 * feature)
    return pl.pallas_call(
        functools.partial(spatial_kernel, scale=scale),
        grid_spec=pltpu.PrefetchScalarGridSpec(
            num_scalar_prefetch=1,
            grid=(frames,),
            in_specs=[
                pl.BlockSpec((1, places, feature), lambda f, s: (f, 0, 0)),
                pl.BlockSpec(kv, lambda f, s: (f, 0, 0)),
                pl.BlockSpec(kv, lambda f, s: (2, 0, 0)),
                pl.BlockSpec(kv, lambda f, s: (jnp.minimum(s[f], 1), 0, 0)),
                pl.BlockSpec(kv, lambda f, s: (jnp.maximum(s[f] - 2, 0), 0, 0)),
                pl.BlockSpec((1, 1, whole), lambda f, s: (0, 0, 0)),
                pl.BlockSpec((1, 1, whole), lambda f, s: (f, 0, 0)),
                pl.BlockSpec((1, places, feature), lambda f, s: (f, 0, 0)),
                pl.BlockSpec((feature, feature), lambda f, s: (0, 0)),
            ],
            out_specs=pl.BlockSpec((1, places, feature), lambda f, s: (f, 0, 0)),
            scratch_shapes=[pltpu.VMEM((places, feature), jnp.bfloat16)],
        ),
        out_shape=jax.ShapeDtypeStruct(video.shape, jnp.bfloat16),
        compiler_params=pltpu.CompilerParams(vmem_limit_bytes=VMEM_BYTES),
        cost_estimate=pl.CostEstimate(
            flops=frames * HEADS * 12 * places * whole * WINDOW,
            bytes_accessed=20 << 20,
            transcendentals=frames * HEADS * places * whole * 3,
        ),
    )(slots, packed, kv_own, kv_rem, kv_rem, kv_own, bias_first, bias_prev, video, wout)


def temporal_rows(rows, open_row, gain, wqkv_ref, wout_ref, pack_ref, mask_ref, att_ref, width, scale):
    count, feature = rows.shape
    normed = normalize(rows.astype(jnp.float32), gain)
    for c in range(3):
        cols = pl.ds(c * feature, feature)
        pack_ref[:, cols] = jnp.dot(
            normed, wqkv_ref[:, cols], preferred_element_type=jnp.float32
        ).astype(jnp.bfloat16)
    i = lax.broadcasted_iota(jnp.int32, (count, count), 0)
    j = lax.broadcasted_iota(jnp.int32, (count, count), 1)
    visible = (i % width == j % width) & ((open_row > 0) | (i == j))
    mask_ref[...] = jnp.where(visible, 0.0, -jnp.inf)
    att_ref[...] = jnp.zeros_like(att_ref)

    def one(head):
        start, inside = head_window(head, feature)
        cols = pl.ds(start, WINDOW)
        kcols = pl.ds(pl.multiple_of(start + feature, 128), WINDOW)
        vcols = pl.ds(pl.multiple_of(start + 2 * feature, 128), WINDOW)
        q = pack_ref[:, cols]
        q = jnp.where(inside, q, jnp.zeros_like(q))
        s = lax.dot_general(
            q, pack_ref[:, kcols], dimension_numbers=NT, preferred_element_type=jnp.float32
        )
        s = s * scale + mask_ref[...]
        p = jnp.exp2(s - jnp.max(s, axis=-1, keepdims=True))
        o = jnp.dot(
            p.astype(jnp.bfloat16), pack_ref[:, vcols], preferred_element_type=jnp.float32
        ) / jnp.sum(p, axis=-1, keepdims=True)
        att_ref[:, cols] = jnp.where(inside, o.astype(jnp.bfloat16), att_ref[:, cols])

    def pair(k, _):
        one(2 * k)
        one(2 * k + 1)
        return 0

    lax.fori_loop(0, HEADS // 2, pair, 0)
    return (
        rows.astype(jnp.float32)
        + jnp.dot(att_ref[...], wout_ref[...], preferred_element_type=jnp.float32)
    ).astype(jnp.bfloat16)


def temporal_kernel(
    rows_ref, open_ref, gain_ref, wqkv_ref, wout_ref, out_ref, pack_ref, mask_ref, att_ref,
    *, width, scale
):
    out_ref[...] = temporal_rows(
        rows_ref[...], open_ref[...], gain_ref[...], wqkv_ref, wout_ref,
        pack_ref, mask_ref, att_ref, width, scale,
    )


def temporal(rows, open_row, gain, wqkv, wout, width, scale):
    count, feature = rows.shape
    return pl.pallas_call(
        functools.partial(temporal_kernel, width=width, scale=scale),
        in_specs=[pl.BlockSpec(memory_space=pltpu.VMEM)] * 5,
        out_specs=pl.BlockSpec(memory_space=pltpu.VMEM),
        out_shape=jax.ShapeDtypeStruct(rows.shape, jnp.bfloat16),
        scratch_shapes=[
            pltpu.VMEM((count, 3 * feature), jnp.bfloat16),
            pltpu.VMEM((count, count), jnp.float32),
            pltpu.VMEM((count, feature), jnp.bfloat16),
        ],
        compiler_params=pltpu.CompilerParams(vmem_limit_bytes=VMEM_BYTES),
        cost_estimate=pl.CostEstimate(
            flops=8 * count * feature * feature, bytes_accessed=12 << 20, transcendentals=0
        ),
    )(rows, open_row, gain, wqkv, wout)


def shards(
    video,
    regions,
    prev_frame,
    gain_spatial,
    qkv_spatial,
    out_spatial,
    gain_temporal,
    qkv_temporal,
    out_temporal,
):
    frames, places, feature = video.shape
    devices = lax.axis_size("frame")
    toks = lax.axis_size("tok")
    total_frames = devices * frames
    whole = toks * places
    scale = (feature // HEADS) ** (-0.5) * math.log2(math.e)

    tail = shifted(video, "frame", 1)
    first = from_root(video[0:1], "frame")
    regions_all = lax.all_gather(regions, ("frame", "tok"), axis=0, tiled=False)
    regions_all = regions_all.reshape(devices, toks, frames, places)
    regions_all = regions_all.transpose(0, 2, 1, 3).reshape(total_frames, whole)

    normed = layer_norm(video.reshape(frames * places, feature), gain_spatial)
    packed = jnp.dot(normed, qkv_spatial, preferred_element_type=jnp.float32).astype(jnp.bfloat16)
    packed = packed.reshape(frames, places, 3 * feature)
    kv_own = lax.all_gather(packed[:, :, feature:], "tok", axis=1, tiled=True)

    remote = jnp.concatenate([tail, first], axis=0)
    normed_r = layer_norm(remote.reshape((frames + 1) * places, feature), gain_spatial)
    kv_rem = jnp.dot(
        normed_r, qkv_spatial[:, feature:], preferred_element_type=jnp.float32
    ).astype(jnp.bfloat16)
    kv_rem = kv_rem.reshape(frames + 1, places, 2 * feature)
    kv_rem = lax.all_gather(kv_rem, "tok", axis=1, tiled=True)

    first_index = lax.axis_index("frame") * frames
    picked = lax.dynamic_slice_in_dim(prev_frame, first_index, frames)
    slots = jnp.clip(picked - first_index + 2, 0, 3).astype(jnp.int32)
    keep_bias = jnp.where(regions_all == 0, 0.0, -jnp.inf).astype(jnp.float32)
    bias_first = keep_bias[0:1][:, None]
    bias_prev = jnp.take(keep_bias, picked, axis=0)[:, None]
    mixed = spatial(
        slots, packed, kv_own, kv_rem, bias_first, bias_prev, video, out_spatial, scale
    )

    width = 16 if places % (devices * 16) == 0 else places // devices
    part = devices * width
    chunks = places // part
    my_open = (regions_all != 2).astype(jnp.float32)
    base = lax.axis_index("tok") * places + lax.axis_index("frame") * width
    gain_row = gain_temporal[None]
    done = []
    for c in range(chunks):
        rows = lax.all_to_all(
            mixed[:, c * part : (c + 1) * part], "frame", split_axis=1, concat_axis=0, tiled=True
        )
        open_row = lax.dynamic_slice_in_dim(my_open, base + c * part, width, axis=1)
        finished = temporal(
            rows.reshape(total_frames * width, feature),
            open_row.reshape(1, total_frames * width),
            gain_row, qkv_temporal, out_temporal, width, scale,
        )
        done.append(
            lax.all_to_all(
                finished.reshape(total_frames, width, feature),
                "frame", split_axis=0, concat_axis=1, tiled=True,
            )
        )
    return jnp.concatenate(done, axis=1)


def solution(mesh):
    placed = (
        P(("groups", "frame"), "tok", None),
        P(("groups", "frame"), "tok"),
        P("groups"),
        P(),
        P(),
        P(),
        P(),
        P(),
        P(),
    )
    return jax.shard_map(
        shards,
        mesh=mesh,
        in_specs=placed,
        out_specs=P(("groups", "frame"), "tok", None),
        check_vma=False,
    )
```

```python
import functools
import math

import jax
import jax.numpy as jnp
from jax import lax
from jax.experimental import pallas as pl
from jax.experimental.pallas import tpu as pltpu
from jax.sharding import PartitionSpec as P

HEADS = 16
WINDOW = 256
VMEM_BYTES = 56 * 1024 * 1024
NT = (((1,), (1,)), ((), ()))


def normalize(values, gain):
    center = values - jnp.mean(values, axis=-1, keepdims=True)
    spread = jnp.mean(center * center, axis=-1, keepdims=True)
    return (center * lax.rsqrt(spread + 1e-06) * gain).astype(jnp.bfloat16)


def head_window(head, feature):
    size = feature // HEADS
    start = jnp.minimum((head * size) // 128 * 128, feature - WINDOW)
    start = pl.multiple_of(start, 128)
    column = lax.broadcasted_iota(jnp.int32, (1, WINDOW), 1) + start
    inside = (column >= head * size) & (column < (head + 1) * size)
    return start, inside


def spatial_kernel(
    slots_ref, video_ref, gain_ref, wqkv_ref, wout_ref, bfirst_ref, bprev_ref, out_ref,
    tail_ref, first_ref, q_ref, own_ref, rem_ref, att_ref,
    scatter_send, spread_send, first_recv, tail_send, tail_recv, kv_send, kv_recv,
    *, devices, scale
):
    frames, places, feature = video_ref.shape
    me = lax.axis_index("frame")
    tok = lax.axis_index("tok")
    piece = places // devices
    mesh_id = pl.DeviceIdType.MESH

    def rows_of(index, size):
        return pl.ds(pl.multiple_of(index * size, size), size)

    mine = rows_of(tok, places)

    barrier = pltpu.get_barrier_semaphore()
    for k in range(1, devices):
        pl.semaphore_signal(
            barrier, inc=1, device_id={"frame": lax.rem(me + k, devices)}, device_id_type=mesh_id
        )
    pl.semaphore_signal(barrier, inc=1, device_id={"tok": 1 - tok}, device_id_type=mesh_id)
    pl.semaphore_wait(barrier, devices)

    def scatter(d):
        return pltpu.make_async_remote_copy(
            src_ref=video_ref.at[0, pl.ds(d * piece, piece)],
            dst_ref=first_ref.at[pl.ds(d * piece, piece)],
            send_sem=scatter_send.at[d],
            recv_sem=first_recv.at[d],
            device_id={"frame": d},
            device_id_type=mesh_id,
        )

    def spread(k):
        return pltpu.make_async_remote_copy(
            src_ref=first_ref.at[rows_of(me, piece)],
            dst_ref=first_ref.at[rows_of(me, piece)],
            send_sem=spread_send.at[k],
            recv_sem=first_recv.at[me],
            device_id={"frame": lax.rem(me + k, devices)},
            device_id_type=mesh_id,
        )

    def arrival(p):
        return pltpu.make_async_remote_copy(
            src_ref=first_ref.at[rows_of(p, piece)],
            dst_ref=first_ref.at[rows_of(p, piece)],
            send_sem=spread_send.at[0],
            recv_sem=first_recv.at[p],
            device_id={"frame": lax.rem(me + 1, devices)},
            device_id_type=mesh_id,
        )

    shift = pltpu.make_async_remote_copy(
        src_ref=video_ref,
        dst_ref=tail_ref,
        send_sem=tail_send,
        recv_sem=tail_recv,
        device_id={"frame": lax.rem(me + 1, devices)},
        device_id_type=mesh_id,
    )

    def swap(ref, index, number):
        return pltpu.make_async_remote_copy(
            src_ref=ref.at[index, mine],
            dst_ref=ref.at[index, mine],
            send_sem=kv_send.at[number],
            recv_sem=kv_recv.at[number],
            device_id={"tok": 1 - tok},
            device_id_type=mesh_id,
        )

    @pl.when(me == 0)
    def _():
        for d in range(1, devices):
            scatter(d).start()
        first_ref[...] = video_ref[0]
        tail_ref[...] = jnp.zeros_like(tail_ref)

    @pl.when(me < devices - 1)
    def _():
        shift.start()

    gain = gain_ref[...]
    keys = pl.ds(feature, feature)
    values = pl.ds(2 * feature, feature)

    def project(normed, cols):
        return jnp.dot(
            normed, wqkv_ref[:, cols], preferred_element_type=jnp.float32
        ).astype(jnp.bfloat16)

    def send_kv(rows, ref, index, number):
        normed = normalize(rows.astype(jnp.float32), gain)
        ref[index, mine, pl.ds(0, feature)] = project(normed, keys)
        ref[index, mine, pl.ds(feature, feature)] = project(normed, values)
        swap(ref, index, number).start()
        return normed

    for f in range(frames):
        normed = send_kv(video_ref[f], own_ref, f, f)
        q_ref[f] = project(normed, pl.ds(0, feature))
        if f == 0:
            @pl.when(me > 0)
            def _():
                arrival(me).wait_recv()

            for k in range(1, devices):
                @pl.when(lax.rem(me + k, devices) != 0)
                def _():
                    spread(k).start()

    @pl.when(me > 0)
    def _():
        shift.wait_recv()

    for f in range(frames):
        send_kv(tail_ref[f], rem_ref, f, frames + f)

    @pl.when(me > 0)
    def _():
        for k in range(1, devices):
            arrival(lax.rem(me + k, devices)).wait_recv()

    send_kv(first_ref[...], rem_ref, frames, 2 * frames)

    for f in range(frames):
        swap(own_ref, f, f).wait()
    for f in range(frames + 1):
        swap(rem_ref, f, frames + f).wait()

    bias_first = bfirst_ref[0]
    att_ref[...] = jnp.zeros_like(att_ref)
    dot = functools.partial(
        lax.dot_general, dimension_numbers=NT, preferred_element_type=jnp.float32
    )
    mul = functools.partial(jnp.dot, preferred_element_type=jnp.float32)

    def frame_step(frame, _):
        slot = slots_ref[frame]
        remote = slot < frames
        rem_slot = jnp.minimum(slot, frames - 1)
        own_slot = jnp.maximum(slot - frames, 0)
        bias_prev = bprev_ref[frame]

        def one(head):
            start, inside = head_window(head, feature)
            cols = pl.ds(start, WINDOW)
            vcols = pl.ds(pl.multiple_of(start + feature, 128), WINDOW)
            q = q_ref[frame, :, cols]
            q = jnp.where(inside, q, jnp.zeros_like(q))

            def prev(c):
                return jnp.where(remote, rem_ref[rem_slot, :, c], own_ref[own_slot, :, c])

            s0 = dot(q, own_ref[frame, :, cols]) * scale
            s1 = dot(q, rem_ref[frames, :, cols]) * scale + bias_first
            s2 = dot(q, prev(cols)) * scale + bias_prev
            m = jnp.max(jnp.maximum(jnp.maximum(s0, s1), s2), axis=-1, keepdims=True)
            p0, p1, p2 = jnp.exp2(s0 - m), jnp.exp2(s1 - m), jnp.exp2(s2 - m)
            total = jnp.sum(p0 + p1 + p2, axis=-1, keepdims=True)
            o = (
                mul(p0.astype(jnp.bfloat16), own_ref[frame, :, vcols])
                + mul(p1.astype(jnp.bfloat16), rem_ref[frames, :, vcols])
                + mul(p2.astype(jnp.bfloat16), prev(vcols))
            ) / total
            att_ref[:, cols] = jnp.where(inside, o.astype(jnp.bfloat16), att_ref[:, cols])

        def pair(i, _):
            one(2 * i)
            one(2 * i + 1)
            return 0

        lax.fori_loop(0, HEADS // 2, pair, 0)
        out_ref[frame] = (
            video_ref[frame].astype(jnp.float32)
            + jnp.dot(att_ref[...], wout_ref[...], preferred_element_type=jnp.float32)
        ).astype(jnp.bfloat16)
        return 0

    lax.fori_loop(0, frames, frame_step, 0)

    @pl.when(me == 0)
    def _():
        for d in range(1, devices):
            scatter(d).wait_send()

    @pl.when(me < devices - 1)
    def _():
        shift.wait_send()

    for k in range(1, devices):
        @pl.when(lax.rem(me + k, devices) != 0)
        def _():
            spread(k).wait_send()


def spatial(slots, video, gain, wqkv, wout, bias_first, bias_prev, devices, toks, scale):
    frames, places, feature = video.shape
    whole = toks * places
    vmem = pl.BlockSpec(memory_space=pltpu.VMEM)
    dma = pltpu.SemaphoreType.DMA
    return pl.pallas_call(
        functools.partial(spatial_kernel, devices=devices, scale=scale),
        in_specs=[pl.BlockSpec(memory_space=pltpu.SMEM)] + [vmem] * 6,
        out_specs=vmem,
        out_shape=jax.ShapeDtypeStruct(video.shape, jnp.bfloat16),
        scratch_shapes=[
            pltpu.VMEM((frames, places, feature), jnp.bfloat16),
            pltpu.VMEM((places, feature), jnp.bfloat16),
            pltpu.VMEM((frames, places, feature), jnp.bfloat16),
            pltpu.VMEM((frames, whole, 2 * feature), jnp.bfloat16),
            pltpu.VMEM((frames + 1, whole, 2 * feature), jnp.bfloat16),
            pltpu.VMEM((places, feature), jnp.bfloat16),
            dma((devices,)),
            dma((devices,)),
            dma((devices,)),
            dma,
            dma,
            dma((2 * frames + 1,)),
            dma((2 * frames + 1,)),
        ],
        compiler_params=pltpu.CompilerParams(
            collective_id=0, has_side_effects=True, vmem_limit_bytes=VMEM_BYTES
        ),
        cost_estimate=pl.CostEstimate(
            flops=frames * HEADS * 12 * places * whole * WINDOW,
            bytes_accessed=20 << 20,
            transcendentals=frames * HEADS * places * whole * 3,
        ),
    )(slots, video, gain, wqkv, wout, bias_first, bias_prev)


def temporal_rows(rows, open_row, gain, wqkv_ref, wout_ref, pack_ref, mask_ref, att_ref, width, scale):
    count, feature = rows.shape
    normed = normalize(rows.astype(jnp.float32), gain)
    for c in range(3):
        cols = pl.ds(c * feature, feature)
        pack_ref[:, cols] = jnp.dot(
            normed, wqkv_ref[:, cols], preferred_element_type=jnp.float32
        ).astype(jnp.bfloat16)
    i = lax.broadcasted_iota(jnp.int32, (count, count), 0)
    j = lax.broadcasted_iota(jnp.int32, (count, count), 1)
    visible = (i % width == j % width) & ((open_row > 0) | (i == j))
    mask_ref[...] = jnp.where(visible, 0.0, -jnp.inf)
    att_ref[...] = jnp.zeros_like(att_ref)

    def one(head):
        start, inside = head_window(head, feature)
        cols = pl.ds(start, WINDOW)
        kcols = pl.ds(pl.multiple_of(start + feature, 128), WINDOW)
        vcols = pl.ds(pl.multiple_of(start + 2 * feature, 128), WINDOW)
        q = pack_ref[:, cols]
        q = jnp.where(inside, q, jnp.zeros_like(q))
        s = lax.dot_general(
            q, pack_ref[:, kcols], dimension_numbers=NT, preferred_element_type=jnp.float32
        )
        s = s * scale + mask_ref[...]
        p = jnp.exp2(s - jnp.max(s, axis=-1, keepdims=True))
        o = jnp.dot(
            p.astype(jnp.bfloat16), pack_ref[:, vcols], preferred_element_type=jnp.float32
        ) / jnp.sum(p, axis=-1, keepdims=True)
        att_ref[:, cols] = jnp.where(inside, o.astype(jnp.bfloat16), att_ref[:, cols])

    def pair(k, _):
        one(2 * k)
        one(2 * k + 1)
        return 0

    lax.fori_loop(0, HEADS // 2, pair, 0)
    return (
        rows.astype(jnp.float32)
        + jnp.dot(att_ref[...], wout_ref[...], preferred_element_type=jnp.float32)
    ).astype(jnp.bfloat16)


def temporal_kernel(
    rows_ref, open_ref, gain_ref, wqkv_ref, wout_ref, out_ref, pack_ref, mask_ref, att_ref,
    *, width, scale
):
    out_ref[...] = temporal_rows(
        rows_ref[...], open_ref[...], gain_ref[...], wqkv_ref, wout_ref,
        pack_ref, mask_ref, att_ref, width, scale,
    )


def temporal(rows, open_row, gain, wqkv, wout, width, scale):
    count, feature = rows.shape
    return pl.pallas_call(
        functools.partial(temporal_kernel, width=width, scale=scale),
        in_specs=[pl.BlockSpec(memory_space=pltpu.VMEM)] * 5,
        out_specs=pl.BlockSpec(memory_space=pltpu.VMEM),
        out_shape=jax.ShapeDtypeStruct(rows.shape, jnp.bfloat16),
        scratch_shapes=[
            pltpu.VMEM((count, 3 * feature), jnp.bfloat16),
            pltpu.VMEM((count, count), jnp.float32),
            pltpu.VMEM((count, feature), jnp.bfloat16),
        ],
        compiler_params=pltpu.CompilerParams(vmem_limit_bytes=VMEM_BYTES),
        cost_estimate=pl.CostEstimate(
            flops=8 * count * feature * feature, bytes_accessed=12 << 20, transcendentals=0
        ),
    )(rows, open_row, gain, wqkv, wout)


def shards(
    video,
    regions,
    prev_frame,
    gain_spatial,
    qkv_spatial,
    out_spatial,
    gain_temporal,
    qkv_temporal,
    out_temporal,
):
    frames, places, feature = video.shape
    devices = lax.axis_size("frame")
    toks = lax.axis_size("tok")
    total_frames = devices * frames
    whole = toks * places
    scale = (feature // HEADS) ** (-0.5) * math.log2(math.e)

    regions_all = lax.all_gather(regions, ("frame", "tok"), axis=0, tiled=False)
    regions_all = regions_all.reshape(devices, toks, frames, places)
    regions_all = regions_all.transpose(0, 2, 1, 3).reshape(total_frames, whole)

    first_index = lax.axis_index("frame") * frames
    picked = lax.dynamic_slice_in_dim(prev_frame, first_index, frames)
    slots = jnp.clip(picked - first_index + frames, 0, 2 * frames - 1).astype(jnp.int32)
    keep_bias = jnp.where(regions_all == 0, 0.0, -jnp.inf).astype(jnp.float32)
    bias_first = keep_bias[0:1][:, None]
    bias_prev = jnp.take(keep_bias, picked, axis=0)[:, None]
    mixed = spatial(
        slots, video, gain_spatial[None], qkv_spatial, out_spatial, bias_first, bias_prev,
        devices, toks, scale,
    )

    width = 16 if places % (devices * 16) == 0 else places // devices
    part = devices * width
    chunks = places // part
    my_open = (regions_all != 2).astype(jnp.float32)
    base = lax.axis_index("tok") * places + lax.axis_index("frame") * width
    gain_row = gain_temporal[None]
    done = []
    for c in range(chunks):
        rows = lax.all_to_all(
            mixed[:, c * part : (c + 1) * part], "frame", split_axis=1, concat_axis=0, tiled=True
        )
        open_row = lax.dynamic_slice_in_dim(my_open, base + c * part, width, axis=1)
        finished = temporal(
            rows.reshape(total_frames * width, feature),
            open_row.reshape(1, total_frames * width),
            gain_row, qkv_temporal, out_temporal, width, scale,
        )
        done.append(
            lax.all_to_all(
                finished.reshape(total_frames, width, feature),
                "frame", split_axis=0, concat_axis=1, tiled=True,
            )
        )
    return jnp.concatenate(done, axis=1)


def solution(mesh):
    placed = (
        P(("groups", "frame"), "tok", None),
        P(("groups", "frame"), "tok"),
        P("groups"),
        P(),
        P(),
        P(),
        P(),
        P(),
        P(),
    )
    return jax.shard_map(
        shards,
        mesh=mesh,
        in_specs=placed,
        out_specs=P(("groups", "frame"), "tok", None),
        check_vma=False,
    )
```

```python
import functools
import math

import jax
import jax.numpy as jnp
from jax import lax
from jax.experimental import pallas as pl
from jax.experimental.pallas import tpu as pltpu
from jax.sharding import PartitionSpec as P

HEADS = 16
WINDOW = 256
VMEM_BYTES = 56 * 1024 * 1024
NT = (((1,), (1,)), ((), ()))


def normalize(values, gain):
    center = values - jnp.mean(values, axis=-1, keepdims=True)
    spread = jnp.mean(center * center, axis=-1, keepdims=True)
    return (center * lax.rsqrt(spread + 1e-06) * gain).astype(jnp.bfloat16)


def head_window(head, feature):
    size = feature // HEADS
    start = jnp.minimum((head * size) // 128 * 128, feature - WINDOW)
    start = pl.multiple_of(start, 128)
    column = lax.broadcasted_iota(jnp.int32, (1, WINDOW), 1) + start
    inside = (column >= head * size) & (column < (head + 1) * size)
    return start, inside


def spatial_kernel(
    slots_ref, video_ref, gain_ref, wqkv_ref, wout_ref, own_reg_ref, out_ref, reg_out_ref,
    tail_ref, first_ref, q_ref, own_ref, rem_ref, att_ref, reg_ref, reg_send, reg_recv,
    scatter_send, spread_send, first_recv, tail_send, tail_recv, kv_send, kv_recv,
    *, devices, scale
):
    frames, places, feature = video_ref.shape
    me = lax.axis_index("frame")
    tok = lax.axis_index("tok")
    piece = places // devices
    mesh_id = pl.DeviceIdType.MESH

    def rows_of(index, size):
        return pl.ds(pl.multiple_of(index * size, size), size)

    mine = rows_of(tok, places)

    barrier = pltpu.get_barrier_semaphore()
    for k in range(1, devices):
        pl.semaphore_signal(
            barrier, inc=1, device_id={"frame": lax.rem(me + k, devices)}, device_id_type=mesh_id
        )
    for k in range(devices):
        pl.semaphore_signal(
            barrier,
            inc=1,
            device_id={"frame": lax.rem(me + k, devices), "tok": 1 - tok},
            device_id_type=mesh_id,
        )
    pl.semaphore_wait(barrier, 2 * devices - 1)

    def tell(j, k):
        return pltpu.make_async_remote_copy(
            src_ref=own_reg_ref,
            dst_ref=reg_ref.at[tok, me],
            send_sem=reg_send.at[j, k],
            recv_sem=reg_recv.at[j, k],
            device_id={"frame": lax.rem(me + k, devices), "tok": tok if j == 0 else 1 - tok},
            device_id_type=mesh_id,
        )

    others = [(j, k) for j in range(2) for k in range(devices) if j + k > 0]

    def scatter(d):
        return pltpu.make_async_remote_copy(
            src_ref=video_ref.at[0, pl.ds(d * piece, piece)],
            dst_ref=first_ref.at[pl.ds(d * piece, piece)],
            send_sem=scatter_send.at[d],
            recv_sem=first_recv.at[d],
            device_id={"frame": d},
            device_id_type=mesh_id,
        )

    def spread(k):
        return pltpu.make_async_remote_copy(
            src_ref=first_ref.at[rows_of(me, piece)],
            dst_ref=first_ref.at[rows_of(me, piece)],
            send_sem=spread_send.at[k],
            recv_sem=first_recv.at[me],
            device_id={"frame": lax.rem(me + k, devices)},
            device_id_type=mesh_id,
        )

    def arrival(p):
        return pltpu.make_async_remote_copy(
            src_ref=first_ref.at[rows_of(p, piece)],
            dst_ref=first_ref.at[rows_of(p, piece)],
            send_sem=spread_send.at[0],
            recv_sem=first_recv.at[p],
            device_id={"frame": lax.rem(me + 1, devices)},
            device_id_type=mesh_id,
        )

    shift = pltpu.make_async_remote_copy(
        src_ref=video_ref,
        dst_ref=tail_ref,
        send_sem=tail_send,
        recv_sem=tail_recv,
        device_id={"frame": lax.rem(me + 1, devices)},
        device_id_type=mesh_id,
    )

    def swap(ref, index, number):
        return pltpu.make_async_remote_copy(
            src_ref=ref.at[index, mine],
            dst_ref=ref.at[index, mine],
            send_sem=kv_send.at[number],
            recv_sem=kv_recv.at[number],
            device_id={"tok": 1 - tok},
            device_id_type=mesh_id,
        )

    @pl.when(me == 0)
    def _():
        for d in range(1, devices):
            scatter(d).start()
        first_ref[...] = video_ref[0]
        tail_ref[...] = jnp.zeros_like(tail_ref)

    @pl.when(me < devices - 1)
    def _():
        shift.start()

    for j, k in others:
        tell(j, k).start()
    reg_ref[tok, me] = own_reg_ref[...]

    gain = gain_ref[...]
    keys = pl.ds(feature, feature)
    values = pl.ds(2 * feature, feature)

    def project(normed, cols):
        return jnp.dot(
            normed, wqkv_ref[:, cols], preferred_element_type=jnp.float32
        ).astype(jnp.bfloat16)

    def send_kv(rows, ref, index, number):
        normed = normalize(rows.astype(jnp.float32), gain)
        ref[index, mine, pl.ds(0, feature)] = project(normed, keys)
        ref[index, mine, pl.ds(feature, feature)] = project(normed, values)
        swap(ref, index, number).start()
        return normed

    for f in range(frames):
        normed = send_kv(video_ref[f], own_ref, f, f)
        q_ref[f] = project(normed, pl.ds(0, feature))
        if f == 0:
            @pl.when(me > 0)
            def _():
                arrival(me).wait_recv()

            for k in range(1, devices):
                @pl.when(lax.rem(me + k, devices) != 0)
                def _():
                    spread(k).start()

    @pl.when(me > 0)
    def _():
        shift.wait_recv()

    for f in range(frames):
        send_kv(tail_ref[f], rem_ref, f, frames + f)

    @pl.when(me > 0)
    def _():
        for k in range(1, devices):
            arrival(lax.rem(me + k, devices)).wait_recv()

    send_kv(first_ref[...], rem_ref, frames, 2 * frames)

    for f in range(frames):
        swap(own_ref, f, f).wait()
    for f in range(frames + 1):
        swap(rem_ref, f, frames + f).wait()

    for j, k in others:
        tell(j, k).wait()
    reg_out_ref[...] = reg_ref[tok]

    def keep_bias(device, row):
        flags = jnp.concatenate([reg_ref[0, device, row], reg_ref[1, device, row]], axis=-1)
        return jnp.where(flags == 0, 0.0, -jnp.inf)

    bias_first = keep_bias(0, 0)
    att_ref[...] = jnp.zeros_like(att_ref)
    dot = functools.partial(
        lax.dot_general, dimension_numbers=NT, preferred_element_type=jnp.float32
    )
    mul = functools.partial(jnp.dot, preferred_element_type=jnp.float32)

    def frame_step(frame, _):
        slot = slots_ref[0, frame]
        remote = slot < frames
        rem_slot = jnp.minimum(slot, frames - 1)
        own_slot = jnp.maximum(slot - frames, 0)
        bias_prev = keep_bias(slots_ref[1, frame], slots_ref[2, frame])

        def one(head):
            start, inside = head_window(head, feature)
            cols = pl.ds(start, WINDOW)
            vcols = pl.ds(pl.multiple_of(start + feature, 128), WINDOW)
            q = q_ref[frame, :, cols]
            q = jnp.where(inside, q, jnp.zeros_like(q))

            def prev(c):
                return jnp.where(remote, rem_ref[rem_slot, :, c], own_ref[own_slot, :, c])

            s0 = dot(q, own_ref[frame, :, cols]) * scale
            s1 = dot(q, rem_ref[frames, :, cols]) * scale + bias_first
            s2 = dot(q, prev(cols)) * scale + bias_prev
            m = jnp.max(jnp.maximum(jnp.maximum(s0, s1), s2), axis=-1, keepdims=True)
            p0, p1, p2 = jnp.exp2(s0 - m), jnp.exp2(s1 - m), jnp.exp2(s2 - m)
            total = jnp.sum(p0 + p1 + p2, axis=-1, keepdims=True)
            o = (
                mul(p0.astype(jnp.bfloat16), own_ref[frame, :, vcols])
                + mul(p1.astype(jnp.bfloat16), rem_ref[frames, :, vcols])
                + mul(p2.astype(jnp.bfloat16), prev(vcols))
            ) / total
            att_ref[:, cols] = jnp.where(inside, o.astype(jnp.bfloat16), att_ref[:, cols])

        def pair(i, _):
            one(2 * i)
            one(2 * i + 1)
            return 0

        lax.fori_loop(0, HEADS // 2, pair, 0)
        out_ref[frame] = (
            video_ref[frame].astype(jnp.float32)
            + jnp.dot(att_ref[...], wout_ref[...], preferred_element_type=jnp.float32)
        ).astype(jnp.bfloat16)
        return 0

    lax.fori_loop(0, frames, frame_step, 0)

    @pl.when(me == 0)
    def _():
        for d in range(1, devices):
            scatter(d).wait_send()

    @pl.when(me < devices - 1)
    def _():
        shift.wait_send()

    for k in range(1, devices):
        @pl.when(lax.rem(me + k, devices) != 0)
        def _():
            spread(k).wait_send()


def spatial(slots, video, gain, wqkv, wout, own_reg, devices, toks, scale):
    frames, places, feature = video.shape
    whole = toks * places
    vmem = pl.BlockSpec(memory_space=pltpu.VMEM)
    dma = pltpu.SemaphoreType.DMA
    return pl.pallas_call(
        functools.partial(spatial_kernel, devices=devices, scale=scale),
        in_specs=[pl.BlockSpec(memory_space=pltpu.SMEM)] + [vmem] * 5,
        out_specs=[vmem, vmem],
        out_shape=[
            jax.ShapeDtypeStruct(video.shape, jnp.bfloat16),
            jax.ShapeDtypeStruct((devices, frames, 1, places), jnp.float32),
        ],
        scratch_shapes=[
            pltpu.VMEM((frames, places, feature), jnp.bfloat16),
            pltpu.VMEM((places, feature), jnp.bfloat16),
            pltpu.VMEM((frames, places, feature), jnp.bfloat16),
            pltpu.VMEM((frames, whole, 2 * feature), jnp.bfloat16),
            pltpu.VMEM((frames + 1, whole, 2 * feature), jnp.bfloat16),
            pltpu.VMEM((places, feature), jnp.bfloat16),
            pltpu.VMEM((toks, devices, frames, 1, places), jnp.float32),
            dma((2, devices)),
            dma((2, devices)),
            dma((devices,)),
            dma((devices,)),
            dma((devices,)),
            dma,
            dma,
            dma((2 * frames + 1,)),
            dma((2 * frames + 1,)),
        ],
        compiler_params=pltpu.CompilerParams(
            collective_id=0, has_side_effects=True, vmem_limit_bytes=VMEM_BYTES
        ),
        cost_estimate=pl.CostEstimate(
            flops=frames * HEADS * 12 * places * whole * WINDOW,
            bytes_accessed=20 << 20,
            transcendentals=frames * HEADS * places * whole * 3,
        ),
    )(slots, video, gain, wqkv, wout, own_reg)


def temporal_rows(rows, open_row, gain, wqkv_ref, wout_ref, pack_ref, mask_ref, att_ref, width, scale):
    count, feature = rows.shape
    normed = normalize(rows.astype(jnp.float32), gain)
    for c in range(3):
        cols = pl.ds(c * feature, feature)
        pack_ref[:, cols] = jnp.dot(
            normed, wqkv_ref[:, cols], preferred_element_type=jnp.float32
        ).astype(jnp.bfloat16)
    i = lax.broadcasted_iota(jnp.int32, (count, count), 0)
    j = lax.broadcasted_iota(jnp.int32, (count, count), 1)
    visible = (i % width == j % width) & ((open_row > 0) | (i == j))
    mask_ref[...] = jnp.where(visible, 0.0, -jnp.inf)
    att_ref[...] = jnp.zeros_like(att_ref)

    def one(head):
        start, inside = head_window(head, feature)
        cols = pl.ds(start, WINDOW)
        kcols = pl.ds(pl.multiple_of(start + feature, 128), WINDOW)
        vcols = pl.ds(pl.multiple_of(start + 2 * feature, 128), WINDOW)
        q = pack_ref[:, cols]
        q = jnp.where(inside, q, jnp.zeros_like(q))
        s = lax.dot_general(
            q, pack_ref[:, kcols], dimension_numbers=NT, preferred_element_type=jnp.float32
        )
        s = s * scale + mask_ref[...]
        p = jnp.exp2(s - jnp.max(s, axis=-1, keepdims=True))
        o = jnp.dot(
            p.astype(jnp.bfloat16), pack_ref[:, vcols], preferred_element_type=jnp.float32
        ) / jnp.sum(p, axis=-1, keepdims=True)
        att_ref[:, cols] = jnp.where(inside, o.astype(jnp.bfloat16), att_ref[:, cols])

    def pair(k, _):
        one(2 * k)
        one(2 * k + 1)
        return 0

    lax.fori_loop(0, HEADS // 2, pair, 0)
    return (
        rows.astype(jnp.float32)
        + jnp.dot(att_ref[...], wout_ref[...], preferred_element_type=jnp.float32)
    ).astype(jnp.bfloat16)


def temporal_kernel(
    mixed_ref, open_ref, gain_ref, wqkv_ref, wout_ref, out_ref,
    recv_ref, fin_ref, land_ref, pack_ref, mask_ref, att_ref,
    go_send, go_recv, back_send, back_recv, *, devices, width, scale
):
    frames, places, feature = mixed_ref.shape
    chunks = recv_ref.shape[0]
    part = devices * width
    count = part * frames
    me = lax.axis_index("frame")
    mesh_id = pl.DeviceIdType.MESH

    barrier = pltpu.get_barrier_semaphore()
    for k in range(1, devices):
        pl.semaphore_signal(
            barrier, inc=1, device_id={"frame": lax.rem(me + k, devices)}, device_id_type=mesh_id
        )
    pl.semaphore_wait(barrier, devices - 1)

    def slab(c, device):
        return pl.ds(pl.multiple_of(c * part + device * width, width), width)

    def go(c, k):
        target = lax.rem(me + k, devices)
        return pltpu.make_async_remote_copy(
            src_ref=mixed_ref.at[:, slab(c, target)],
            dst_ref=recv_ref.at[c, me],
            send_sem=go_send.at[c, k],
            recv_sem=go_recv.at[c, k],
            device_id={"frame": target},
            device_id_type=mesh_id,
        )

    def back(c, k):
        target = lax.rem(me + k, devices)
        return pltpu.make_async_remote_copy(
            src_ref=fin_ref.at[c, target],
            dst_ref=land_ref.at[:, slab(c, me)],
            send_sem=back_send.at[c, k],
            recv_sem=back_recv.at[c, k],
            device_id={"frame": target},
            device_id_type=mesh_id,
        )

    for c in range(chunks):
        for k in range(1, devices):
            go(c, k).start()
        recv_ref[c, me] = mixed_ref[:, slab(c, me)]
    for c in range(chunks):
        for k in range(1, devices):
            go(c, k).wait()
        finished = temporal_rows(
            recv_ref[c].reshape(count, feature), open_ref[c], gain_ref[...], wqkv_ref, wout_ref,
            pack_ref, mask_ref, att_ref, width, scale,
        )
        fin_ref[c] = finished.reshape(devices, frames, width, feature)
        for k in range(1, devices):
            back(c, k).start()
        land_ref[:, slab(c, me)] = fin_ref[c, me]
    for c in range(chunks):
        for k in range(1, devices):
            back(c, k).wait()
    out_ref[...] = land_ref[...]


def temporal(mixed, open_rows, gain, wqkv, wout, devices, width, scale):
    frames, places, feature = mixed.shape
    chunks, _, count = open_rows.shape
    vmem = pl.BlockSpec(memory_space=pltpu.VMEM)
    block = pltpu.VMEM((chunks, devices, frames, width, feature), jnp.bfloat16)
    return pl.pallas_call(
        functools.partial(temporal_kernel, devices=devices, width=width, scale=scale),
        in_specs=[vmem] * 5,
        out_specs=vmem,
        out_shape=jax.ShapeDtypeStruct(mixed.shape, jnp.bfloat16),
        scratch_shapes=[
            block,
            block,
            pltpu.VMEM(mixed.shape, jnp.bfloat16),
            pltpu.VMEM((count, 3 * feature), jnp.bfloat16),
            pltpu.VMEM((count, count), jnp.float32),
            pltpu.VMEM((count, feature), jnp.bfloat16),
        ]
        + [pltpu.SemaphoreType.DMA((chunks, devices))] * 4,
        compiler_params=pltpu.CompilerParams(
            collective_id=1, has_side_effects=True, vmem_limit_bytes=VMEM_BYTES
        ),
        cost_estimate=pl.CostEstimate(
            flops=8 * chunks * count * feature * feature,
            bytes_accessed=16 << 20,
            transcendentals=0,
        ),
    )(mixed, open_rows, gain, wqkv, wout)


def shards(
    video,
    regions,
    prev_frame,
    gain_spatial,
    qkv_spatial,
    out_spatial,
    gain_temporal,
    qkv_temporal,
    out_temporal,
):
    frames, places, feature = video.shape
    devices = lax.axis_size("frame")
    toks = lax.axis_size("tok")
    total_frames = devices * frames
    whole = toks * places
    scale = (feature // HEADS) ** (-0.5) * math.log2(math.e)

    first_index = lax.axis_index("frame") * frames
    picked = lax.dynamic_slice_in_dim(prev_frame, first_index, frames)
    slots = jnp.clip(picked - first_index + frames, 0, 2 * frames - 1).astype(jnp.int32)
    slots = jnp.stack([slots, picked // frames, picked % frames])
    own_reg = regions.astype(jnp.float32)[:, None]
    mixed, known = spatial(
        slots, video, gain_spatial[None], qkv_spatial, out_spatial, own_reg, devices, toks, scale
    )
    width = 16 if places % (devices * 16) == 0 else places // devices
    part = devices * width
    chunks = places // part
    is_open = (known.reshape(total_frames, places) != 2).astype(jnp.float32)
    base = lax.axis_index("frame") * width
    open_rows = jnp.stack(
        [
            lax.dynamic_slice_in_dim(is_open, base + c * part, width, axis=1).reshape(1, -1)
            for c in range(chunks)
        ]
    )
    return temporal(
        mixed, open_rows, gain_temporal[None], qkv_temporal, out_temporal, devices, width, scale
    )


def solution(mesh):
    placed = (
        P(("groups", "frame"), "tok", None),
        P(("groups", "frame"), "tok"),
        P("groups"),
        P(),
        P(),
        P(),
        P(),
        P(),
        P(),
    )
    return jax.shard_map(
        shards,
        mesh=mesh,
        in_specs=placed,
        out_specs=P(("groups", "frame"), "tok", None),
        check_vma=False,
    )
```

```python
import functools
import math

import jax
import jax.numpy as jnp
from jax import lax
from jax.experimental import pallas as pl
from jax.experimental.pallas import tpu as pltpu
from jax.sharding import PartitionSpec as P

HEADS = 16
WINDOW = 256
VMEM_BYTES = 56 * 1024 * 1024
NT = (((1,), (1,)), ((), ()))


def normalize(values, gain):
    center = values - jnp.mean(values, axis=-1, keepdims=True)
    spread = jnp.mean(center * center, axis=-1, keepdims=True)
    return (center * lax.rsqrt(spread + 1e-06) * gain).astype(jnp.bfloat16)


def head_window(head, feature):
    size = feature // HEADS
    start = jnp.minimum((head * size) // 128 * 128, feature - WINDOW)
    start = pl.multiple_of(start, 128)
    column = lax.broadcasted_iota(jnp.int32, (1, WINDOW), 1) + start
    inside = (column >= head * size) & (column < (head + 1) * size)
    return start, inside


def spatial_kernel(
    slots_ref, video_ref, gain_ref, wqkv_ref, wout_ref, own_reg_ref, out_ref, reg_out_ref,
    tail_ref, first_ref, q_ref, own_ref, rem_ref, att_ref, reg_ref, reg_send, reg_recv,
    scatter_send, spread_send, first_recv, tail_send, tail_recv, kv_send, kv_recv,
    *, devices, scale
):
    frames, places, feature = video_ref.shape
    me = lax.axis_index("frame")
    tok = lax.axis_index("tok")
    piece = places // devices
    mesh_id = pl.DeviceIdType.MESH

    def rows_of(index, size):
        return pl.ds(pl.multiple_of(index * size, size), size)

    mine = rows_of(tok, places)

    barrier = pltpu.get_barrier_semaphore()
    for k in range(1, devices):
        pl.semaphore_signal(
            barrier, inc=1, device_id={"frame": lax.rem(me + k, devices)}, device_id_type=mesh_id
        )
    for k in range(devices):
        pl.semaphore_signal(
            barrier,
            inc=1,
            device_id={"frame": lax.rem(me + k, devices), "tok": 1 - tok},
            device_id_type=mesh_id,
        )
    pl.semaphore_wait(barrier, 2 * devices - 1)

    def tell(j, k):
        return pltpu.make_async_remote_copy(
            src_ref=own_reg_ref,
            dst_ref=reg_ref.at[tok, me],
            send_sem=reg_send.at[j, k],
            recv_sem=reg_recv.at[j, k],
            device_id={"frame": lax.rem(me + k, devices), "tok": tok if j == 0 else 1 - tok},
            device_id_type=mesh_id,
        )

    others = [(j, k) for j in range(2) for k in range(devices) if j + k > 0]

    def scatter(d):
        return pltpu.make_async_remote_copy(
            src_ref=video_ref.at[0, pl.ds(d * piece, piece)],
            dst_ref=first_ref.at[pl.ds(d * piece, piece)],
            send_sem=scatter_send.at[d],
            recv_sem=first_recv.at[d],
            device_id={"frame": d},
            device_id_type=mesh_id,
        )

    def spread(k):
        return pltpu.make_async_remote_copy(
            src_ref=first_ref.at[rows_of(me, piece)],
            dst_ref=first_ref.at[rows_of(me, piece)],
            send_sem=spread_send.at[k],
            recv_sem=first_recv.at[me],
            device_id={"frame": lax.rem(me + k, devices)},
            device_id_type=mesh_id,
        )

    def arrival(p):
        return pltpu.make_async_remote_copy(
            src_ref=first_ref.at[rows_of(p, piece)],
            dst_ref=first_ref.at[rows_of(p, piece)],
            send_sem=spread_send.at[0],
            recv_sem=first_recv.at[p],
            device_id={"frame": lax.rem(me + 1, devices)},
            device_id_type=mesh_id,
        )

    shift = pltpu.make_async_remote_copy(
        src_ref=video_ref,
        dst_ref=tail_ref,
        send_sem=tail_send,
        recv_sem=tail_recv,
        device_id={"frame": lax.rem(me + 1, devices)},
        device_id_type=mesh_id,
    )

    def swap(ref, index, number):
        return pltpu.make_async_remote_copy(
            src_ref=ref.at[index, mine],
            dst_ref=ref.at[index, mine],
            send_sem=kv_send.at[number],
            recv_sem=kv_recv.at[number],
            device_id={"tok": 1 - tok},
            device_id_type=mesh_id,
        )

    @pl.when(me == 0)
    def _():
        for d in range(1, devices):
            scatter(d).start()
        first_ref[...] = video_ref[0]
        tail_ref[...] = jnp.zeros_like(tail_ref)

    @pl.when(me < devices - 1)
    def _():
        shift.start()

    for j, k in others:
        tell(j, k).start()
    reg_ref[tok, me] = own_reg_ref[...]

    gain = gain_ref[...]
    keys = pl.ds(feature, feature)
    values = pl.ds(2 * feature, feature)

    def project(normed, cols):
        return jnp.dot(
            normed, wqkv_ref[:, cols], preferred_element_type=jnp.float32
        ).astype(jnp.bfloat16)

    def send_kv(rows, ref, index, number):
        normed = normalize(rows.astype(jnp.float32), gain)
        ref[index, mine, pl.ds(0, feature)] = project(normed, keys)
        ref[index, mine, pl.ds(feature, feature)] = project(normed, values)
        swap(ref, index, number).start()
        return normed

    for f in range(frames):
        normed = send_kv(video_ref[f], own_ref, f, f)
        q_ref[f] = project(normed, pl.ds(0, feature))
        if f == 0:
            @pl.when(me > 0)
            def _():
                arrival(me).wait_recv()

            for k in range(1, devices):
                @pl.when(lax.rem(me + k, devices) != 0)
                def _():
                    spread(k).start()

    @pl.when(me > 0)
    def _():
        for k in range(1, devices):
            arrival(lax.rem(me + k, devices)).wait_recv()

    send_kv(first_ref[...], rem_ref, frames, 2 * frames)

    @pl.when(me > 0)
    def _():
        shift.wait_recv()

    for f in range(frames):
        send_kv(tail_ref[f], rem_ref, f, frames + f)

    for f in range(frames):
        swap(own_ref, f, f).wait()
    for f in range(frames + 1):
        swap(rem_ref, f, frames + f).wait()

    for j, k in others:
        tell(j, k).wait()
    reg_out_ref[...] = reg_ref[tok]

    def keep_bias(device, row):
        flags = jnp.concatenate([reg_ref[0, device, row], reg_ref[1, device, row]], axis=-1)
        return jnp.where(flags == 0, 0.0, -jnp.inf)

    bias_first = keep_bias(0, 0)
    att_ref[...] = jnp.zeros_like(att_ref)
    dot = functools.partial(
        lax.dot_general, dimension_numbers=NT, preferred_element_type=jnp.float32
    )
    mul = functools.partial(jnp.dot, preferred_element_type=jnp.float32)

    def frame_step(frame, _):
        slot = slots_ref[0, frame]
        remote = slot < frames
        rem_slot = jnp.minimum(slot, frames - 1)
        own_slot = jnp.maximum(slot - frames, 0)
        bias_prev = keep_bias(slots_ref[1, frame], slots_ref[2, frame])

        def one(head):
            start, inside = head_window(head, feature)
            cols = pl.ds(start, WINDOW)
            vcols = pl.ds(pl.multiple_of(start + feature, 128), WINDOW)
            q = q_ref[frame, :, cols]
            q = jnp.where(inside, q, jnp.zeros_like(q))

            def prev(c):
                return jnp.where(remote, rem_ref[rem_slot, :, c], own_ref[own_slot, :, c])

            s0 = dot(q, own_ref[frame, :, cols]) * scale
            s1 = dot(q, rem_ref[frames, :, cols]) * scale + bias_first
            s2 = dot(q, prev(cols)) * scale + bias_prev
            m = jnp.max(jnp.maximum(jnp.maximum(s0, s1), s2), axis=-1, keepdims=True)
            p0, p1, p2 = jnp.exp2(s0 - m), jnp.exp2(s1 - m), jnp.exp2(s2 - m)
            total = jnp.sum(p0 + p1 + p2, axis=-1, keepdims=True)
            o = (
                mul(p0.astype(jnp.bfloat16), own_ref[frame, :, vcols])
                + mul(p1.astype(jnp.bfloat16), rem_ref[frames, :, vcols])
                + mul(p2.astype(jnp.bfloat16), prev(vcols))
            ) / total
            att_ref[:, cols] = jnp.where(inside, o.astype(jnp.bfloat16), att_ref[:, cols])

        def group(i, _):
            for extra in range(4):
                one(4 * i + extra)
            return 0

        lax.fori_loop(0, HEADS // 4, group, 0)
        out_ref[frame] = (
            video_ref[frame].astype(jnp.float32)
            + jnp.dot(att_ref[...], wout_ref[...], preferred_element_type=jnp.float32)
        ).astype(jnp.bfloat16)
        return 0

    lax.fori_loop(0, frames, frame_step, 0)

    @pl.when(me == 0)
    def _():
        for d in range(1, devices):
            scatter(d).wait_send()

    @pl.when(me < devices - 1)
    def _():
        shift.wait_send()

    for k in range(1, devices):
        @pl.when(lax.rem(me + k, devices) != 0)
        def _():
            spread(k).wait_send()


def spatial(slots, video, gain, wqkv, wout, own_reg, devices, toks, scale):
    frames, places, feature = video.shape
    whole = toks * places
    vmem = pl.BlockSpec(memory_space=pltpu.VMEM)
    dma = pltpu.SemaphoreType.DMA
    return pl.pallas_call(
        functools.partial(spatial_kernel, devices=devices, scale=scale),
        in_specs=[pl.BlockSpec(memory_space=pltpu.SMEM)] + [vmem] * 5,
        out_specs=[vmem, vmem],
        out_shape=[
            jax.ShapeDtypeStruct(video.shape, jnp.bfloat16),
            jax.ShapeDtypeStruct((devices, frames, 1, places), jnp.float32),
        ],
        scratch_shapes=[
            pltpu.VMEM((frames, places, feature), jnp.bfloat16),
            pltpu.VMEM((places, feature), jnp.bfloat16),
            pltpu.VMEM((frames, places, feature), jnp.bfloat16),
            pltpu.VMEM((frames, whole, 2 * feature), jnp.bfloat16),
            pltpu.VMEM((frames + 1, whole, 2 * feature), jnp.bfloat16),
            pltpu.VMEM((places, feature), jnp.bfloat16),
            pltpu.VMEM((toks, devices, frames, 1, places), jnp.float32),
            dma((2, devices)),
            dma((2, devices)),
            dma((devices,)),
            dma((devices,)),
            dma((devices,)),
            dma,
            dma,
            dma((2 * frames + 1,)),
            dma((2 * frames + 1,)),
        ],
        compiler_params=pltpu.CompilerParams(
            collective_id=0, has_side_effects=True, vmem_limit_bytes=VMEM_BYTES
        ),
        cost_estimate=pl.CostEstimate(
            flops=frames * HEADS * 12 * places * whole * WINDOW,
            bytes_accessed=20 << 20,
            transcendentals=frames * HEADS * places * whole * 3,
        ),
    )(slots, video, gain, wqkv, wout, own_reg)


def temporal_rows(rows, open_row, gain, wqkv_ref, wout_ref, pack_ref, mask_ref, att_ref, width, scale):
    count, feature = rows.shape
    normed = normalize(rows.astype(jnp.float32), gain)
    for c in range(3):
        cols = pl.ds(c * feature, feature)
        pack_ref[:, cols] = jnp.dot(
            normed, wqkv_ref[:, cols], preferred_element_type=jnp.float32
        ).astype(jnp.bfloat16)
    i = lax.broadcasted_iota(jnp.int32, (count, count), 0)
    j = lax.broadcasted_iota(jnp.int32, (count, count), 1)
    visible = (i % width == j % width) & ((open_row > 0) | (i == j))
    mask_ref[...] = jnp.where(visible, 0.0, -jnp.inf)
    att_ref[...] = jnp.zeros_like(att_ref)

    def one(head):
        start, inside = head_window(head, feature)
        cols = pl.ds(start, WINDOW)
        kcols = pl.ds(pl.multiple_of(start + feature, 128), WINDOW)
        vcols = pl.ds(pl.multiple_of(start + 2 * feature, 128), WINDOW)
        q = pack_ref[:, cols]
        q = jnp.where(inside, q, jnp.zeros_like(q))
        s = lax.dot_general(
            q, pack_ref[:, kcols], dimension_numbers=NT, preferred_element_type=jnp.float32
        )
        s = s * scale + mask_ref[...]
        p = jnp.exp2(s - jnp.max(s, axis=-1, keepdims=True))
        o = jnp.dot(
            p.astype(jnp.bfloat16), pack_ref[:, vcols], preferred_element_type=jnp.float32
        ) / jnp.sum(p, axis=-1, keepdims=True)
        att_ref[:, cols] = jnp.where(inside, o.astype(jnp.bfloat16), att_ref[:, cols])

    def group(k, _):
        for extra in range(4):
            one(4 * k + extra)
        return 0

    lax.fori_loop(0, HEADS // 4, group, 0)
    return (
        rows.astype(jnp.float32)
        + jnp.dot(att_ref[...], wout_ref[...], preferred_element_type=jnp.float32)
    ).astype(jnp.bfloat16)


def temporal_kernel(
    mixed_ref, open_ref, gain_ref, wqkv_ref, wout_ref, out_ref,
    recv_ref, fin_ref, land_ref, pack_ref, mask_ref, att_ref,
    go_send, go_recv, back_send, back_recv, *, devices, width, scale
):
    frames, places, feature = mixed_ref.shape
    chunks = recv_ref.shape[0]
    part = devices * width
    count = part * frames
    me = lax.axis_index("frame")
    mesh_id = pl.DeviceIdType.MESH

    barrier = pltpu.get_barrier_semaphore()
    for k in range(1, devices):
        pl.semaphore_signal(
            barrier, inc=1, device_id={"frame": lax.rem(me + k, devices)}, device_id_type=mesh_id
        )
    pl.semaphore_wait(barrier, devices - 1)

    def slab(c, device):
        return pl.ds(pl.multiple_of(c * part + device * width, width), width)

    def go(c, k):
        target = lax.rem(me + k, devices)
        return pltpu.make_async_remote_copy(
            src_ref=mixed_ref.at[:, slab(c, target)],
            dst_ref=recv_ref.at[c, me],
            send_sem=go_send.at[c, k],
            recv_sem=go_recv.at[c, k],
            device_id={"frame": target},
            device_id_type=mesh_id,
        )

    def back(c, k):
        target = lax.rem(me + k, devices)
        return pltpu.make_async_remote_copy(
            src_ref=fin_ref.at[c, target],
            dst_ref=land_ref.at[:, slab(c, me)],
            send_sem=back_send.at[c, k],
            recv_sem=back_recv.at[c, k],
            device_id={"frame": target},
            device_id_type=mesh_id,
        )

    for c in range(chunks):
        for k in range(1, devices):
            go(c, k).start()
        recv_ref[c, me] = mixed_ref[:, slab(c, me)]
    for c in range(chunks):
        for k in range(1, devices):
            go(c, k).wait()
        finished = temporal_rows(
            recv_ref[c].reshape(count, feature), open_ref[c], gain_ref[...], wqkv_ref, wout_ref,
            pack_ref, mask_ref, att_ref, width, scale,
        )
        fin_ref[c] = finished.reshape(devices, frames, width, feature)
        for k in range(1, devices):
            back(c, k).start()
        land_ref[:, slab(c, me)] = fin_ref[c, me]
    for c in range(chunks):
        for k in range(1, devices):
            back(c, k).wait()
    out_ref[...] = land_ref[...]


def temporal(mixed, open_rows, gain, wqkv, wout, devices, width, scale):
    frames, places, feature = mixed.shape
    chunks, _, count = open_rows.shape
    vmem = pl.BlockSpec(memory_space=pltpu.VMEM)
    block = pltpu.VMEM((chunks, devices, frames, width, feature), jnp.bfloat16)
    return pl.pallas_call(
        functools.partial(temporal_kernel, devices=devices, width=width, scale=scale),
        in_specs=[vmem] * 5,
        out_specs=vmem,
        out_shape=jax.ShapeDtypeStruct(mixed.shape, jnp.bfloat16),
        scratch_shapes=[
            block,
            block,
            pltpu.VMEM(mixed.shape, jnp.bfloat16),
            pltpu.VMEM((count, 3 * feature), jnp.bfloat16),
            pltpu.VMEM((count, count), jnp.float32),
            pltpu.VMEM((count, feature), jnp.bfloat16),
        ]
        + [pltpu.SemaphoreType.DMA((chunks, devices))] * 4,
        compiler_params=pltpu.CompilerParams(
            collective_id=1, has_side_effects=True, vmem_limit_bytes=VMEM_BYTES
        ),
        cost_estimate=pl.CostEstimate(
            flops=8 * chunks * count * feature * feature,
            bytes_accessed=16 << 20,
            transcendentals=0,
        ),
    )(mixed, open_rows, gain, wqkv, wout)


def shards(
    video,
    regions,
    prev_frame,
    gain_spatial,
    qkv_spatial,
    out_spatial,
    gain_temporal,
    qkv_temporal,
    out_temporal,
):
    frames, places, feature = video.shape
    devices = lax.axis_size("frame")
    toks = lax.axis_size("tok")
    total_frames = devices * frames
    whole = toks * places
    scale = (feature // HEADS) ** (-0.5) * math.log2(math.e)

    first_index = lax.axis_index("frame") * frames
    picked = lax.dynamic_slice_in_dim(prev_frame, first_index, frames)
    slots = jnp.clip(picked - first_index + frames, 0, 2 * frames - 1).astype(jnp.int32)
    slots = jnp.stack([slots, picked // frames, picked % frames])
    own_reg = regions.astype(jnp.float32)[:, None]
    mixed, known = spatial(
        slots, video, gain_spatial[None], qkv_spatial, out_spatial, own_reg, devices, toks, scale
    )
    width = 16 if places % (devices * 16) == 0 else places // devices
    part = devices * width
    chunks = places // part
    is_open = (known.reshape(total_frames, places) != 2).astype(jnp.float32)
    base = lax.axis_index("frame") * width
    open_rows = jnp.stack(
        [
            lax.dynamic_slice_in_dim(is_open, base + c * part, width, axis=1).reshape(1, -1)
            for c in range(chunks)
        ]
    )
    return temporal(
        mixed, open_rows, gain_temporal[None], qkv_temporal, out_temporal, devices, width, scale
    )


def solution(mesh):
    placed = (
        P(("groups", "frame"), "tok", None),
        P(("groups", "frame"), "tok"),
        P("groups"),
        P(),
        P(),
        P(),
        P(),
        P(),
        P(),
    )
    return jax.shard_map(
        shards,
        mesh=mesh,
        in_specs=placed,
        out_specs=P(("groups", "frame"), "tok", None),
        check_vma=False,
    )
```
